32 devices in a mesh: grp: 2 (over x), loop: 16 (over z, y, core).
Axes of the slice: x: 2, y: 2, z: 4, core: 2. Of those that a mesh axis runs over, the one named last changes fastest.
Arguments:
- rows_in: bfloat16 [512, 6144], P(('grp', 'loop')), parts along dimension 0, may hold values from -6 to 6
- rows_grad: bfloat16 [512, 6144], P(('grp', 'loop')), parts along dimension 0, may hold values from -6 to 6
- route_weight: float32 [512, 2], P('grp'), parts along dimension 0, may hold values from 0.1 to 0.9
- expert_ids: int32 [512, 2], P('grp'), parts along dimension 0, may hold values from 0 to 7, all different within a row; in each aligned block of 256 rows (0 to 255, 256 to 511, ...) at most 128 rows name the same one
- w_gate: bfloat16 [6144, 16384], P(None, 'loop'), may hold values from -0.078125 to 0.078125
- w_up: bfloat16 [6144, 16384], P(None, 'loop'), may hold values from -0.078125 to 0.078125
- w_down: bfloat16 [16384, 6144], P('loop'), may hold values from -0.046875 to 0.046875
- delta_in: bfloat16 [2048, 6144], P('loop'), may hold values from -0.078125 to 0.078125
- delta_out: bfloat16 [2048, 6144], P('loop'), may hold values from -0.375 to 0.375
Outputs:
- grad_rows: bfloat16 [512, 6144], P(('grp', 'loop')), parts along dimension 0
- grad_gate: bfloat16 [12288, 16384], P('grp', 'loop'), parts along dimension 0
- grad_up: bfloat16 [12288, 16384], P('grp', 'loop'), parts along dimension 0
- grad_down: bfloat16 [32768, 6144], P(('grp', 'loop')), parts along dimension 0
- grad_delta_in: bfloat16 [4096, 6144], P(('grp', 'loop')), parts along dimension 0
- grad_delta_out: bfloat16 [4096, 6144], P(('grp', 'loop')), parts along dimension 0
The draws below stay inside these ranges and needn't reach their ends.
There are 2 independent parts, one for each index of `grp`. The reference program is written for one: setup_inputs(seed, part) draws one part's arguments, and reference() takes and returns one part's arrays. A program takes and returns all parts, laid end to end along the dimension named above; an argument that names none is the same for every part. Nothing has to cross between parts.
Inputs may be any that keep to these rules, and one draw needn't show every extreme that they name: `expert_ids`: each row names 2 different experts; every expert is named by some row; no expert is named by more than 128 rows, a bound that some block reaches.
All inputs are finite; a program needn't handle non-finite values.
Results may differ from the reference program's by a relative error of at most 0.005.
Values may be sent and summed in bfloat16 or wider, within the bound.
A program may use at most 192 MiB of HBM per device.

```python
import math
import jax
import jax.numpy as jnp
import numpy as np

D = 6144
FF = 16384
EXPERTS = 8
RANK = 256
TOP = 2
TOKENS = 256
CAPACITY = 128


def steps_of(rng, shape, shards, least, top_value):
    def one(position, blocks):
        steps = jax.random.uniform(jax.random.fold_in(jax.random.fold_in(rng, 6), position), (blocks,), jnp.float32, least / len(shards), top_value / len(shards))
        return jnp.repeat(jnp.exp(steps), shape[position] // blocks).reshape((-1,) + (1,) * (len(shape) - position - 1))

    gain = one(*shards[0])
    for cut in shards[1:]:
        gain = gain * one(*cut)
    return gain


def shared_out(key, own, number, rows, amount, top, limit, lean):
    sequence = jax.random.permutation(key, amount)
    heavy_load, common = load_shares(amount, rows * top, limit, lean, True), load_shares(amount, rows * top, limit, lean, False)
    places = jnp.arange(amount)

    def named(tallies, turn):
        used = int((tallies > 0).sum())
        fixed = max(1, used // 4)
        passed = fixed + (places - fixed + turn * (used - fixed)) % max(1, amount - fixed)
        return jnp.zeros((amount,), jnp.int32).at[sequence[jnp.where(places < fixed, places, passed)]].set(jnp.asarray(tallies, jnp.int32))

    tallies = jnp.where(number % 4 == 0, named(heavy_load, number // 4), named(common, number - number // 4 - 1))
    mixed = jax.random.permutation(jax.random.fold_in(own, 3), amount)
    giver, taker = mixed[0:amount // 2 * 2:2], mixed[1:amount // 2 * 2:2]
    slack = jnp.minimum(tallies[giver] - 1, limit - tallies[taker]) // 2
    slack = jnp.where((giver == sequence[0]) | (taker == sequence[0]) | (tallies[taker] == 0), 0, jnp.maximum(slack, 0))
    passed = jax.random.randint(jax.random.fold_in(own, 4), (amount // 2,), 0, 1 << 20) % (slack + 1)
    tallies = tallies.at[giver].add(-passed).at[taker].add(passed)
    members = jnp.searchsorted(jnp.cumsum(tallies), jnp.arange(rows * top), side="right").astype(jnp.int32)
    table = members.reshape(top, rows).T
    table = table[jax.random.permutation(jax.random.fold_in(own, 1), rows)]
    turn = jax.random.randint(jax.random.fold_in(own, 2), (rows, 1), 0, top)
    return jnp.take_along_axis(table, (jnp.arange(top)[None, :] + turn) % top, axis=1)


def load_shares(number_of, total, limit, lean, full):
    weights = [(1 << 20) // math.isqrt(rank ** lean) + 1 for rank in range(1, number_of + 1)]
    largest = limit if full else min(limit, max(-(-total // number_of), total * weights[0] // sum(weights)))
    least = 1 if total - largest >= number_of - 1 else 0
    counts, spare = [largest] + [least] * (number_of - 1), total - largest - least * (number_of - 1)
    while spare > 0:
        candidates = [i for i in range(1, number_of) if counts[i] < largest] or [i for i in range(1, number_of) if counts[i] < limit]
        mass, left = sum([weights[i] for i in candidates]), spare
        for i in candidates:
            extra = min(limit - counts[i], max(1, left * weights[i] // mass), spare)
            counts[i] = counts[i] + extra
            spare = spare - extra
    return np.array(counts)


def scatter_about(stream_key, extent, deviation, bound, pieces=(), kind=jnp.bfloat16):
    values = jax.random.normal(stream_key, extent, jnp.float32) * deviation
    if len(pieces) > 0:
        values = steps_of(stream_key, extent, pieces, -0.22, 0.18) * values
    return jnp.clip(values, min=-bound, max=bound).astype(kind)


def setup_inputs(seed: int = 0, part: int = 0) -> dict:
    keys = jax.random.split(jax.random.key(seed), 10)
    own_keys = jax.random.split(jax.random.fold_in(keys[9], part), 10)
    rows_in = scatter_about(own_keys[0], (TOKENS, D), 1.0, 6.0, ((0, 16),))
    rows_grad = scatter_about(own_keys[1], (TOKENS, D), 1.0, 6.0, ((0, 16),))
    route_weight = jnp.clip(jax.random.uniform(own_keys[2], (TOKENS, TOP), jnp.float32, 0.1, 0.9), 0.1, 0.9)
    expert_ids_keys = jax.random.split(jax.random.fold_in(own_keys[3], 1), TOKENS // TOKENS)
    expert_ids_turns = jax.random.permutation(jax.random.fold_in(own_keys[3], 3), TOKENS // TOKENS)
    expert_ids = jax.vmap(lambda own, number: shared_out(jax.random.fold_in(own_keys[3], 2), own, number, TOKENS, EXPERTS, TOP, CAPACITY, 2))(expert_ids_keys, expert_ids_turns).reshape((TOKENS, TOP))
    w_gate = scatter_about(keys[4], (D, FF), D ** -0.5, 0.078125, ((1, 16),))
    w_up = scatter_about(keys[5], (D, FF), D ** -0.5, 0.078125, ((1, 16),))
    w_down = scatter_about(keys[6], (FF, D), FF ** -0.5, 0.046875, ((0, 16),))
    delta_in = scatter_about(keys[7], (EXPERTS * RANK, D), D ** -0.5, 0.078125, ((0, 16),))
    delta_out = scatter_about(keys[8], (EXPERTS * RANK, D), RANK ** -0.5, 0.375, ((0, 16),))
    return dict(rows_in=rows_in, rows_grad=rows_grad, route_weight=route_weight, expert_ids=expert_ids, w_gate=w_gate, w_up=w_up, w_down=w_down, delta_in=delta_in, delta_out=delta_out)


def reference(rows_in, rows_grad, route_weight, expert_ids, w_gate, w_up, w_down, delta_in, delta_out):
    gate = jnp.dot(rows_in, w_gate, preferred_element_type=jnp.float32)
    up = jnp.dot(rows_in, w_up, preferred_element_type=jnp.float32)
    sig = jax.nn.sigmoid(gate)
    hidden = (gate * sig * up).astype(jnp.bfloat16)
    grad_hidden = jnp.dot(rows_grad, w_down.T, preferred_element_type=jnp.float32)
    grad_pre_gate = (grad_hidden * up * sig * (1.0 + gate * (1.0 - sig))).astype(jnp.bfloat16)
    grad_pre_up = (grad_hidden * gate * sig).astype(jnp.bfloat16)
    grad_down = jnp.dot(hidden.T, rows_grad, preferred_element_type=jnp.float32).astype(jnp.bfloat16)
    grad_gate = jnp.dot(rows_in.T, grad_pre_gate, preferred_element_type=jnp.float32).astype(jnp.bfloat16)
    grad_up = jnp.dot(rows_in.T, grad_pre_up, preferred_element_type=jnp.float32).astype(jnp.bfloat16)
    total = jnp.dot(grad_pre_gate, w_gate.T, preferred_element_type=jnp.float32)
    total = total + jnp.dot(grad_pre_up, w_up.T, preferred_element_type=jnp.float32)
    in_parts = []
    out_parts = []
    for expert in range(EXPERTS):
        coef = jnp.sum(jnp.where(expert_ids == expert, route_weight, jnp.zeros_like(route_weight)), axis=1)
        map_in = delta_in[expert * RANK:(expert + 1) * RANK]
        map_out = delta_out[expert * RANK:(expert + 1) * RANK]
        proj = jnp.dot(rows_in, map_in.T, preferred_element_type=jnp.float32)
        back = jnp.dot(rows_grad, map_out.T, preferred_element_type=jnp.float32)
        grad_z = (coef[:, None] * back).astype(jnp.bfloat16)
        scaled_z = (coef[:, None] * proj).astype(jnp.bfloat16)
        in_parts.append(jnp.dot(grad_z.T, rows_in, preferred_element_type=jnp.float32).astype(jnp.bfloat16))
        out_parts.append(jnp.dot(scaled_z.T, rows_grad, preferred_element_type=jnp.float32).astype(jnp.bfloat16))
        total = total + jnp.dot(grad_z, map_in, preferred_element_type=jnp.float32)
    grad_rows = total.astype(jnp.bfloat16)
    return (grad_rows, grad_gate, grad_up, grad_down, jnp.concatenate(in_parts, axis=0), jnp.concatenate(out_parts, axis=0))
```

```python
import functools

import jax
import jax.numpy as jnp
from jax import lax
from jax.experimental import pallas as pl
from jax.experimental.pallas import tpu as pltpu
from jax.sharding import PartitionSpec as P

RANK = 256
BF = jnp.bfloat16
F32 = jnp.float32
MESH = pl.DeviceIdType.MESH
NT = (((1,), (1,)), ((), ()))
TN = (((0,), (0,)), ((), ()))


def dot_nt(a, b):
    return lax.dot_general(a, b, NT, preferred_element_type=F32)


def dot_tn(a, b):
    return lax.dot_general(a, b, TN, preferred_element_type=F32)


def forward_kernel(
    chunks,
    rows_in, rows_grad, coef, w_gate, w_up, w_down, delta_in, delta_out,
    grad_rows, x_out, g_out, hid_out, gpg_out, gpu_out, dz_out, cz_out,
    act, wg, wu, wd, din, dout, fac_a, fac_b, hid, gpg, gpu, dz, cz,
    part, c_in, c_sum, y_in, y_sum, z_in,
    load_sem, own_sem, out_sem, send_sem, recv_sem,
    c_send, c_recv, y_send, y_recv, z_send, z_recv,
):
    me = lax.axis_index("loop")
    z, y, c = me // 4, (me // 2) % 2, me % 2
    rows = rows_in.shape[0]
    tile = 256
    width = part.shape[-1]

    def zpeer(d):
        return ((z // 2 + d // 2) % 2) * 2 + (z % 2 + d % 2) % 2

    def ident(zz, yy, cc):
        return zz * 4 + yy * 2 + cc

    loads = [
        pltpu.make_async_copy(w_gate, wg, load_sem.at[0]),
        pltpu.make_async_copy(w_up, wu, load_sem.at[1]),
        pltpu.make_async_copy(delta_in, din, load_sem.at[2]),
        pltpu.make_async_copy(w_down, wd, load_sem.at[3]),
        pltpu.make_async_copy(delta_out, dout, load_sem.at[4]),
    ]
    own = [
        pltpu.make_async_copy(src, act.at[a, pl.ds(me * rows, rows)], own_sem.at[a])
        for a, src in enumerate((rows_in, rows_grad))
    ]
    for cp in own + loads:
        cp.start()

    barrier = pltpu.get_barrier_semaphore()
    for d in range(1, 4):
        pl.semaphore_signal(
            barrier, inc=1, device_id={"loop": ident(zpeer(d), y, c)}, device_id_type=MESH
        )
    pl.semaphore_signal(barrier, inc=1, device_id={"loop": ident(z, 1 - y, c)}, device_id_type=MESH)
    pl.semaphore_signal(barrier, inc=1, device_id={"loop": ident(z, y, 1 - c)}, device_id_type=MESH)
    pl.semaphore_wait(barrier, 5)

    def block_copy(a, block, target, slot):
        ref = act.at[a, pl.ds(block * rows, rows)]
        return pltpu.make_async_remote_copy(
            src_ref=ref, dst_ref=ref, send_sem=send_sem.at[a, slot], recv_sem=recv_sem.at[a, block],
            device_id={"loop": target}, device_id_type=MESH,
        )

    def to_z(a, d):
        return block_copy(a, me, ident(zpeer(d), y, c), d - 1)

    def to_y(a, d):
        return block_copy(a, ident(zpeer(d), y, c), ident(z, 1 - y, c), 3 + d)

    def to_core(a, d, yy, slot):
        return block_copy(a, ident(zpeer(d), yy, c), ident(z, y, 1 - c), slot)

    def arrived(a, block):
        block_copy(a, block, me + 1 - 2 * c, 0).wait_recv()

    for a in range(2):
        own[a].wait()
        to_y(a, 0).start()
        for d in range(1, 4):
            to_z(a, d).start()
        to_core(a, 0, y, 7).start()

    def relay(a, j):
        @pl.when(j < 3)
        def _():
            arrived(a, ident(zpeer(j + 1), y, c))
            to_y(a, j + 1).start()
            to_core(a, j + 1, y, 8 + j).start()

        arrived(a, ident(zpeer(j), 1 - y, c))
        to_core(a, j, 1 - y, 11 + j).start()

    def settle(a):
        @pl.loop(0, 4)
        def _(j):
            arrived(a, ident(zpeer(j), y, 1 - c))
            arrived(a, ident(zpeer(j), 1 - y, 1 - c))

    @pl.loop(0, 4)
    def _(j):
        relay(0, j)

    settle(0)
    x_copy = pltpu.make_async_copy(act.at[0], x_out, out_sem.at[0])
    x_copy.start()
    loads[0].wait()
    loads[1].wait()
    loads[2].wait()

    n_tiles = hid.shape[1] // tile

    @pl.loop(0, n_tiles)
    def _(j):
        cols = pl.ds(pl.multiple_of(j * tile, tile), tile)
        gate = jnp.dot(act[0], wg[:, cols], preferred_element_type=F32)
        up = jnp.dot(act[0], wu[:, cols], preferred_element_type=F32)
        sig = jax.nn.sigmoid(gate)
        silu = gate * sig
        hid[:, cols] = (silu * up).astype(BF)
        fac_b[:, cols] = silu
        fac_a[:, cols] = up * sig * (1.0 + gate * (1.0 - sig))

        @pl.when(j < 4)
        def _():
            relay(1, j)

    proj = dot_nt(act[0], din[...])
    cz[...] = (coef[...] * proj).astype(BF)
    settle(1)
    g_copy = pltpu.make_async_copy(act.at[1], g_out, out_sem.at[1])
    g_copy.start()
    loads[3].wait()
    loads[4].wait()
    back = dot_nt(act[1], dout[...])
    dz[...] = (coef[...] * back).astype(BF)

    @pl.loop(0, n_tiles)
    def _(j):
        cols = pl.ds(pl.multiple_of(j * tile, tile), tile)
        grad_hidden = dot_nt(act[1], wd[cols, :])
        gpg[:, cols] = (grad_hidden * fac_a[:, cols]).astype(BF)
        gpu[:, cols] = (grad_hidden * fac_b[:, cols]).astype(BF)

    outs = [
        pltpu.make_async_copy(src, dst, out_sem.at[2 + i])
        for i, (src, dst) in enumerate(
            ((hid, hid_out), (gpg, gpg_out), (gpu, gpu_out), (dz, dz_out), (cz, cz_out))
        )
    ]
    for cp in outs:
        cp.start()

    def c_copy(s):
        return pltpu.make_async_remote_copy(
            src_ref=part.at[s, :, 1 - c], dst_ref=c_in.at[s], send_sem=c_send.at[s],
            recv_sem=c_recv.at[s], device_id={"loop": ident(z, y, 1 - c)}, device_id_type=MESH,
        )

    def y_copy(s):
        return pltpu.make_async_remote_copy(
            src_ref=c_sum.at[s, :, 1 - y], dst_ref=y_in.at[s], send_sem=y_send.at[s],
            recv_sem=y_recv.at[s], device_id={"loop": ident(z, 1 - y, c)}, device_id_type=MESH,
        )

    def z_copy(s, d):
        return pltpu.make_async_remote_copy(
            src_ref=y_sum.at[s, zpeer(d)], dst_ref=z_in.at[s, d - 1], send_sem=z_send.at[s, d - 1],
            recv_sem=z_recv.at[s, d - 1], device_id={"loop": ident(zpeer(d), y, c)},
            device_id_type=MESH,
        )

    @pl.loop(0, chunks + 3)
    def _(s):
        @pl.when(s < chunks)
        def _():
            cols = pl.ds(pl.multiple_of(s * width, width), width)
            total = dot_nt(gpg[...], wg[cols, :]) + dot_nt(gpu[...], wu[cols, :])
            total = total + jnp.dot(dz[...], din[:, cols], preferred_element_type=F32)
            part[s] = total.astype(BF).reshape(part.shape[1:])
            c_copy(s).start()

        @pl.when((s >= 1) & (s < chunks + 1))
        def _():
            t = s - 1
            c_copy(t).wait_recv()
            add = part[t, :, c].astype(F32) + c_in[t].astype(F32)
            c_sum[t] = add.astype(BF).reshape(c_sum.shape[1:])
            y_copy(t).start()

        @pl.when((s >= 2) & (s < chunks + 2))
        def _():
            t = s - 2
            y_copy(t).wait_recv()
            y_sum[t] = (c_sum[t, :, y].astype(F32) + y_in[t].astype(F32)).astype(BF)
            for d in range(1, 4):
                z_copy(t, d).start()

        @pl.when(s >= 3)
        def _():
            t = s - 3
            total = y_sum[t, z].astype(F32)
            for d in range(1, 4):
                z_copy(t, d).wait_recv()
                total = total + z_in[t, d - 1].astype(F32)
            cols = pl.ds(pl.multiple_of(t * width, width), width)
            grad_rows[:, cols] = total.astype(BF)

    @pl.loop(0, chunks)
    def _(s):
        c_copy(s).wait_send()
        y_copy(s).wait_send()
        for d in range(1, 4):
            z_copy(s, d).wait_send()

    for a in range(2):
        for slot in range(15):
            block_copy(a, me, me + 1 - 2 * c, slot).wait_send()
    x_copy.wait()
    g_copy.wait()
    for cp in outs:
        cp.wait()


def forward(rows_in, rows_grad, coef, w_gate, w_up, w_down, delta_in, delta_out):
    rows, d = rows_in.shape
    tokens = rows * 16
    ff = w_gate.shape[1]
    own = delta_in.shape[0]
    width = 1024
    chunks = d // width
    sds = jax.ShapeDtypeStruct
    dma = pltpu.SemaphoreType.DMA
    vmem = pltpu.VMEM
    hbm = pl.BlockSpec(memory_space=pl.ANY)
    return pl.pallas_call(
        functools.partial(forward_kernel, chunks),
        out_shape=(
            sds((rows, d), BF), sds((tokens, d), BF), sds((tokens, d), BF),
            sds((tokens, ff), BF), sds((tokens, ff), BF), sds((tokens, ff), BF),
            sds((tokens, own), BF), sds((tokens, own), BF),
        ),
        in_specs=[hbm, hbm, pl.BlockSpec(memory_space=pltpu.VMEM)] + [hbm] * 5,
        out_specs=[pl.BlockSpec(memory_space=pltpu.VMEM)] + [hbm] * 7,
        scratch_shapes=[
            vmem((2, tokens, d), BF), vmem((d, ff), BF), vmem((d, ff), BF), vmem((ff, d), BF),
            vmem((own, d), BF), vmem((own, d), BF),
            vmem((tokens, ff), F32), vmem((tokens, ff), F32),
            vmem((tokens, ff), BF), vmem((tokens, ff), BF), vmem((tokens, ff), BF),
            vmem((tokens, own), BF), vmem((tokens, own), BF),
            vmem((chunks, 8, 2, rows, width), BF), vmem((chunks, 8, rows, width), BF),
            vmem((chunks, 4, 2, rows, width), BF), vmem((chunks, 4, rows, width), BF),
            vmem((chunks, 4, rows, width), BF), vmem((chunks, 3, rows, width), BF),
            dma((5,)), dma((2,)), dma((7,)), dma((2, 15)), dma((2, 16)),
            dma((chunks,)), dma((chunks,)), dma((chunks,)), dma((chunks,)),
            dma((chunks, 3)), dma((chunks, 3)),
        ],
        compiler_params=pltpu.CompilerParams(
            collective_id=0, has_side_effects=True, vmem_limit_bytes=63 * 1024 * 1024
        ),
        cost_estimate=pl.CostEstimate(
            flops=2 * tokens * d * (5 * ff + 3 * own), bytes_accessed=2 * d * (3 * ff + 3 * tokens),
            transcendentals=tokens * ff,
        ),
    )(rows_in, rows_grad, coef, w_gate, w_up, w_down, delta_in, delta_out)


def weight_kernel(x, g, hid, gpg, gpu, dz, cz, o_gate, o_up, o_down, o_in, o_out):
    xt = x[...].T
    o_gate[...] = jnp.dot(xt, gpg[...], preferred_element_type=F32).astype(BF)
    o_up[...] = jnp.dot(xt, gpu[...], preferred_element_type=F32).astype(BF)
    o_down[...] = dot_tn(hid[...], g[...]).astype(BF)
    o_in[...] = dot_tn(dz[...], x[...]).astype(BF)
    o_out[...] = dot_tn(cz[...], g[...]).astype(BF)


def weight_grads(x, g, hid, gpg, gpu, dz, cz):
    tokens, d = x.shape
    ff, own = hid.shape[1], dz.shape[1]
    step = 512
    sds = jax.ShapeDtypeStruct
    full = lambda n: pl.BlockSpec((tokens, n), lambda i: (0, 0))
    part = pl.BlockSpec((tokens, step), lambda i: (0, i))
    tall = pl.BlockSpec((step, ff), lambda i: (i, 0))
    return pl.pallas_call(
        weight_kernel,
        grid=(d // step,),
        out_shape=(sds((d, ff), BF), sds((d, ff), BF), sds((ff, d), BF), sds((own, d), BF), sds((own, d), BF)),
        in_specs=[part, part, full(ff), full(ff), full(ff), full(own), full(own)],
        out_specs=[tall, tall] + [pl.BlockSpec((n, step), lambda i: (0, i)) for n in (ff, own, own)],
        compiler_params=pltpu.CompilerParams(vmem_limit_bytes=56 * 1024 * 1024),
        cost_estimate=pl.CostEstimate(
            flops=2 * tokens * d * (3 * ff + 2 * own), bytes_accessed=2 * d * (3 * ff + 2 * own + 2 * tokens),
            transcendentals=0,
        ),
    )(x, g, hid, gpg, gpu, dz, cz)


def coef_of(route_weight, expert_ids, owned):
    expert = lax.axis_index("loop") * owned // RANK
    matched = expert_ids == expert
    return jnp.sum(jnp.where(matched, route_weight, jnp.zeros_like(route_weight)), axis=1)


def fused_device(
    rows_in, rows_grad, route_weight, expert_ids, w_gate, w_up, w_down, delta_in, delta_out
):
    owned = delta_in.shape[0]
    coef = coef_of(route_weight, expert_ids, owned)
    coef = jnp.broadcast_to(coef[:, None], (coef.shape[0], owned))
    grad_rows, x, g, hid, gpg, gpu, dz, cz = forward(
        rows_in, rows_grad, coef, w_gate, w_up, w_down, delta_in, delta_out
    )
    return (grad_rows,) + tuple(weight_grads(x, g, hid, gpg, gpu, dz, cz))


def per_device(
    rows_in, rows_grad, route_weight, expert_ids, w_gate, w_up, w_down, delta_in, delta_out
):
    inputs, cotangent = (
        lax.all_gather(rows_in, "loop", axis=0, tiled=True),
        lax.all_gather(rows_grad, "loop", axis=0, tiled=True),
    )
    gate = jnp.dot(inputs, w_gate, preferred_element_type=jnp.float32)
    up = jnp.dot(inputs, w_up, preferred_element_type=jnp.float32)
    sig = jax.nn.sigmoid(gate)
    hidden = (gate * sig * up).astype(jnp.bfloat16)
    grad_hidden = jnp.dot(cotangent, w_down.T, preferred_element_type=jnp.float32)
    grad_pre_gate = (grad_hidden * up * sig * (1.0 + gate * (1.0 - sig))).astype(jnp.bfloat16)
    grad_pre_up = (grad_hidden * gate * sig).astype(jnp.bfloat16)
    grad_down = jnp.dot(hidden.T, cotangent, preferred_element_type=jnp.float32).astype(
        jnp.bfloat16
    )
    grad_gate = jnp.dot(inputs.T, grad_pre_gate, preferred_element_type=jnp.float32).astype(
        jnp.bfloat16
    )
    grad_up = jnp.dot(inputs.T, grad_pre_up, preferred_element_type=jnp.float32).astype(
        jnp.bfloat16
    )
    owned = delta_in.shape[0]
    expert = lax.axis_index("loop") * owned // RANK
    matched = expert_ids == expert
    coef = jnp.sum(jnp.where(matched, route_weight, jnp.zeros_like(route_weight)), axis=1)
    proj = jnp.dot(inputs, delta_in.T, preferred_element_type=jnp.float32)
    back = jnp.dot(cotangent, delta_out.T, preferred_element_type=jnp.float32)
    grad_z = (coef[:, None] * back).astype(jnp.bfloat16)
    scaled_z = (coef[:, None] * proj).astype(jnp.bfloat16)
    grad_delta_in = jnp.dot(grad_z.T, inputs, preferred_element_type=jnp.float32).astype(
        jnp.bfloat16
    )
    grad_delta_out = jnp.dot(scaled_z.T, cotangent, preferred_element_type=jnp.float32).astype(
        jnp.bfloat16
    )
    delta_rows_term = jnp.dot(grad_z, delta_in, preferred_element_type=jnp.float32)
    partial_value = jnp.dot(grad_pre_gate, w_gate.T, preferred_element_type=jnp.float32)
    partial_value = partial_value + jnp.dot(grad_pre_up, w_up.T, preferred_element_type=jnp.float32)
    partial_value = partial_value + delta_rows_term
    summed = lax.psum_scatter(partial_value, "loop", scatter_dimension=0, tiled=True)
    grad_rows = summed.astype(jnp.bfloat16)
    return (grad_rows, grad_gate, grad_up, grad_down, grad_delta_in, grad_delta_out)


def solution(mesh):
    placed = (
        P(("grp", "loop"), None),
        P(("grp", "loop"), None),
        P("grp", None),
        P("grp", None),
        P(None, "loop"),
        P(None, "loop"),
        P("loop", None),
        P("loop", None),
        P("loop", None),
    )
    device = fused_device if mesh.shape["loop"] == 16 else per_device
    return jax.shard_map(
        device,
        mesh=mesh,
        in_specs=placed,
        out_specs=(
            P(("grp", "loop"), None),
            P("grp", "loop"),
            P("grp", "loop"),
            P(("grp", "loop"), None),
            P(("grp", "loop"), None),
            P(("grp", "loop"), None),
        ),
        check_vma=False,
    )
```

```python
import functools

import jax
import jax.numpy as jnp
from jax import lax
from jax.experimental import pallas as pl
from jax.experimental.pallas import tpu as pltpu
from jax.sharding import PartitionSpec as P

RANK = 256
BF = jnp.bfloat16
F32 = jnp.float32
MESH = pl.DeviceIdType.MESH
NT = (((1,), (1,)), ((), ()))
TN = (((0,), (0,)), ((), ()))


def dot_nt(a, b):
    return lax.dot_general(a, b, NT, preferred_element_type=F32)


def dot_tn(a, b):
    return lax.dot_general(a, b, TN, preferred_element_type=F32)


def forward_kernel(
    chunks,
    rows_in, rows_grad, route_weight, expert_ids, w_gate, w_up, w_down, delta_in, delta_out,
    grad_rows, x_out, g_out, hid_out, gpg_out, gpu_out, dz_out, cz_out,
    act, wg, wu, wd, din, dout, fac_a, fac_b, hid, gpg, gpu, dz, cz,
    part, c_in, c_sum, y_in, y_sum, z_in,
    load_sem, own_sem, out_sem, send_sem, recv_sem,
    c_send, c_recv, y_send, y_recv, z_send, z_recv,
):
    me = lax.axis_index("loop")
    z, y, c = me // 4, (me // 2) % 2, me % 2
    rows = rows_in.shape[0]
    tile = 256
    width = part.shape[-1]

    def zpeer(d):
        return ((z // 2 + d // 2) % 2) * 2 + (z % 2 + d % 2) % 2

    def ident(zz, yy, cc):
        return zz * 4 + yy * 2 + cc

    loads = [
        pltpu.make_async_copy(w_gate, wg, load_sem.at[0]),
        pltpu.make_async_copy(w_up, wu, load_sem.at[1]),
        pltpu.make_async_copy(delta_in, din, load_sem.at[2]),
        pltpu.make_async_copy(w_down, wd, load_sem.at[3]),
        pltpu.make_async_copy(delta_out, dout, load_sem.at[4]),
    ]
    own = [
        pltpu.make_async_copy(src, act.at[a, pl.ds(me * rows, rows)], own_sem.at[a])
        for a, src in enumerate((rows_in, rows_grad))
    ]
    for cp in own + loads:
        cp.start()

    barrier = pltpu.get_barrier_semaphore()
    for d in range(1, 4):
        pl.semaphore_signal(
            barrier, inc=1, device_id={"loop": ident(zpeer(d), y, c)}, device_id_type=MESH
        )
    pl.semaphore_signal(barrier, inc=1, device_id={"loop": ident(z, 1 - y, c)}, device_id_type=MESH)
    pl.semaphore_signal(barrier, inc=1, device_id={"loop": ident(z, y, 1 - c)}, device_id_type=MESH)
    pl.semaphore_wait(barrier, 5)

    def block_copy(a, block, target, slot):
        ref = act.at[a, pl.ds(block * rows, rows)]
        return pltpu.make_async_remote_copy(
            src_ref=ref, dst_ref=ref, send_sem=send_sem.at[a, slot], recv_sem=recv_sem.at[a, block],
            device_id={"loop": target}, device_id_type=MESH,
        )

    def to_z(a, d):
        return block_copy(a, me, ident(zpeer(d), y, c), d - 1)

    def to_y(a, d):
        return block_copy(a, ident(zpeer(d), y, c), ident(z, 1 - y, c), 3 + d)

    def to_core(a, d, yy, slot):
        return block_copy(a, ident(zpeer(d), yy, c), ident(z, y, 1 - c), slot)

    def arrived(a, block):
        block_copy(a, block, me + 1 - 2 * c, 0).wait_recv()

    for a in range(2):
        own[a].wait()
        to_y(a, 0).start()
        for d in range(1, 4):
            to_z(a, d).start()
        to_core(a, 0, y, 7).start()

    def relay(a, j):
        @pl.when(j < 3)
        def _():
            arrived(a, ident(zpeer(j + 1), y, c))
            to_y(a, j + 1).start()
            to_core(a, j + 1, y, 8 + j).start()

        arrived(a, ident(zpeer(j), 1 - y, c))
        to_core(a, j, 1 - y, 11 + j).start()

    def settle(a):
        @pl.loop(0, 4)
        def _(j):
            arrived(a, ident(zpeer(j), y, 1 - c))
            arrived(a, ident(zpeer(j), 1 - y, 1 - c))

    @pl.loop(0, 4)
    def _(j):
        relay(0, j)

    settle(0)
    x_copy = pltpu.make_async_copy(act.at[0], x_out, out_sem.at[0])
    x_copy.start()
    loads[0].wait()
    loads[1].wait()
    loads[2].wait()

    n_tiles = hid.shape[1] // tile

    @pl.loop(0, n_tiles)
    def _(j):
        cols = pl.ds(pl.multiple_of(j * tile, tile), tile)
        gate = jnp.dot(act[0], wg[:, cols], preferred_element_type=F32)
        up = jnp.dot(act[0], wu[:, cols], preferred_element_type=F32)
        sig = jax.nn.sigmoid(gate)
        silu = gate * sig
        hid[:, cols] = (silu * up).astype(BF)
        fac_b[:, cols] = silu
        fac_a[:, cols] = up * sig * (1.0 + gate * (1.0 - sig))

        @pl.when(j < 4)
        def _():
            relay(1, j)

    matched = expert_ids[...] == me * din.shape[0] // RANK
    coef = jnp.sum(jnp.where(matched, route_weight[...], 0.0), axis=1, keepdims=True)
    proj = dot_nt(act[0], din[...])
    cz[...] = (coef * proj).astype(BF)
    settle(1)
    g_copy = pltpu.make_async_copy(act.at[1], g_out, out_sem.at[1])
    g_copy.start()
    loads[3].wait()
    loads[4].wait()
    back = dot_nt(act[1], dout[...])
    dz[...] = (coef * back).astype(BF)

    @pl.loop(0, n_tiles)
    def _(j):
        cols = pl.ds(pl.multiple_of(j * tile, tile), tile)
        grad_hidden = dot_nt(act[1], wd[cols, :])
        gpg[:, cols] = (grad_hidden * fac_a[:, cols]).astype(BF)
        gpu[:, cols] = (grad_hidden * fac_b[:, cols]).astype(BF)

    outs = [
        pltpu.make_async_copy(src, dst, out_sem.at[2 + i])
        for i, (src, dst) in enumerate(
            ((hid, hid_out), (gpg, gpg_out), (gpu, gpu_out), (dz, dz_out), (cz, cz_out))
        )
    ]
    for cp in outs:
        cp.start()

    def c_copy(s):
        return pltpu.make_async_remote_copy(
            src_ref=part.at[s, :, 1 - c], dst_ref=c_in.at[s], send_sem=c_send.at[s],
            recv_sem=c_recv.at[s], device_id={"loop": ident(z, y, 1 - c)}, device_id_type=MESH,
        )

    def y_copy(s):
        return pltpu.make_async_remote_copy(
            src_ref=c_sum.at[s, :, 1 - y], dst_ref=y_in.at[s], send_sem=y_send.at[s],
            recv_sem=y_recv.at[s], device_id={"loop": ident(z, 1 - y, c)}, device_id_type=MESH,
        )

    def z_copy(s, d):
        return pltpu.make_async_remote_copy(
            src_ref=y_sum.at[s, zpeer(d)], dst_ref=z_in.at[s, d - 1], send_sem=z_send.at[s, d - 1],
            recv_sem=z_recv.at[s, d - 1], device_id={"loop": ident(zpeer(d), y, c)},
            device_id_type=MESH,
        )

    @pl.loop(0, chunks + 3)
    def _(s):
        @pl.when(s < chunks)
        def _():
            cols = pl.ds(pl.multiple_of(s * width, width), width)
            total = dot_nt(gpg[...], wg[cols, :]) + dot_nt(gpu[...], wu[cols, :])
            total = total + jnp.dot(dz[...], din[:, cols], preferred_element_type=F32)
            part[s] = total.astype(BF).reshape(part.shape[1:])
            c_copy(s).start()

        @pl.when((s >= 1) & (s < chunks + 1))
        def _():
            t = s - 1
            c_copy(t).wait_recv()
            add = part[t, :, c].astype(F32) + c_in[t].astype(F32)
            c_sum[t] = add.astype(BF).reshape(c_sum.shape[1:])
            y_copy(t).start()

        @pl.when((s >= 2) & (s < chunks + 2))
        def _():
            t = s - 2
            y_copy(t).wait_recv()
            y_sum[t] = (c_sum[t, :, y].astype(F32) + y_in[t].astype(F32)).astype(BF)
            for d in range(1, 4):
                z_copy(t, d).start()

        @pl.when(s >= 3)
        def _():
            t = s - 3
            total = y_sum[t, z].astype(F32)
            for d in range(1, 4):
                z_copy(t, d).wait_recv()
                total = total + z_in[t, d - 1].astype(F32)
            cols = pl.ds(pl.multiple_of(t * width, width), width)
            grad_rows[:, cols] = total.astype(BF)

    @pl.loop(0, chunks)
    def _(s):
        c_copy(s).wait_send()
        y_copy(s).wait_send()
        for d in range(1, 4):
            z_copy(s, d).wait_send()

    for a in range(2):
        for slot in range(15):
            block_copy(a, me, me + 1 - 2 * c, slot).wait_send()
    x_copy.wait()
    g_copy.wait()
    for cp in outs:
        cp.wait()


def forward(rows_in, rows_grad, route_weight, expert_ids, w_gate, w_up, w_down, delta_in, delta_out):
    rows, d = rows_in.shape
    tokens = rows * 16
    ff = w_gate.shape[1]
    own = delta_in.shape[0]
    width = 1024
    chunks = d // width
    sds = jax.ShapeDtypeStruct
    dma = pltpu.SemaphoreType.DMA
    vmem = pltpu.VMEM
    hbm = pl.BlockSpec(memory_space=pl.ANY)
    return pl.pallas_call(
        functools.partial(forward_kernel, chunks),
        out_shape=(
            sds((rows, d), BF), sds((tokens, d), BF), sds((tokens, d), BF),
            sds((tokens, ff), BF), sds((tokens, ff), BF), sds((tokens, ff), BF),
            sds((tokens, own), BF), sds((tokens, own), BF),
        ),
        in_specs=[hbm] * 2 + [pl.BlockSpec(memory_space=pltpu.VMEM)] * 2 + [hbm] * 5,
        out_specs=[pl.BlockSpec(memory_space=pltpu.VMEM)] + [hbm] * 7,
        scratch_shapes=[
            vmem((2, tokens, d), BF), vmem((d, ff), BF), vmem((d, ff), BF), vmem((ff, d), BF),
            vmem((own, d), BF), vmem((own, d), BF),
            vmem((tokens, ff), F32), vmem((tokens, ff), F32),
            vmem((tokens, ff), BF), vmem((tokens, ff), BF), vmem((tokens, ff), BF),
            vmem((tokens, own), BF), vmem((tokens, own), BF),
            vmem((chunks, 8, 2, rows, width), BF), vmem((chunks, 8, rows, width), BF),
            vmem((chunks, 4, 2, rows, width), BF), vmem((chunks, 4, rows, width), BF),
            vmem((chunks, 4, rows, width), BF), vmem((chunks, 3, rows, width), BF),
            dma((5,)), dma((2,)), dma((7,)), dma((2, 15)), dma((2, 16)),
            dma((chunks,)), dma((chunks,)), dma((chunks,)), dma((chunks,)),
            dma((chunks, 3)), dma((chunks, 3)),
        ],
        compiler_params=pltpu.CompilerParams(
            collective_id=0, has_side_effects=True, vmem_limit_bytes=63 * 1024 * 1024
        ),
        cost_estimate=pl.CostEstimate(
            flops=2 * tokens * d * (5 * ff + 3 * own), bytes_accessed=2 * d * (3 * ff + 3 * tokens),
            transcendentals=tokens * ff,
        ),
    )(rows_in, rows_grad, route_weight, expert_ids, w_gate, w_up, w_down, delta_in, delta_out)


def weight_kernel(x, g, hid, gpg, gpu, dz, cz, o_gate, o_up, o_down, o_in, o_out):
    o_gate[...] = dot_tn(x[...], gpg[...]).astype(BF)
    o_up[...] = dot_tn(x[...], gpu[...]).astype(BF)
    o_down[...] = dot_tn(hid[...], g[...]).astype(BF)
    o_in[...] = dot_tn(dz[...], x[...]).astype(BF)
    o_out[...] = dot_tn(cz[...], g[...]).astype(BF)


def weight_grads(x, g, hid, gpg, gpu, dz, cz):
    tokens, d = x.shape
    ff, own = hid.shape[1], dz.shape[1]
    step = 1024
    sds = jax.ShapeDtypeStruct
    full = lambda n: pl.BlockSpec((tokens, n), lambda i: (0, 0))
    part = pl.BlockSpec((tokens, step), lambda i: (0, i))
    tall = pl.BlockSpec((step, ff), lambda i: (i, 0))
    return pl.pallas_call(
        weight_kernel,
        grid=(d // step,),
        out_shape=(sds((d, ff), BF), sds((d, ff), BF), sds((ff, d), BF), sds((own, d), BF), sds((own, d), BF)),
        in_specs=[part, part, full(ff), full(ff), full(ff), full(own), full(own)],
        out_specs=[tall, tall] + [pl.BlockSpec((n, step), lambda i: (0, i)) for n in (ff, own, own)],
        compiler_params=pltpu.CompilerParams(vmem_limit_bytes=56 * 1024 * 1024),
        cost_estimate=pl.CostEstimate(
            flops=2 * tokens * d * (3 * ff + 2 * own), bytes_accessed=2 * d * (3 * ff + 2 * own + 2 * tokens),
            transcendentals=0,
        ),
    )(x, g, hid, gpg, gpu, dz, cz)


def fused_device(
    rows_in, rows_grad, route_weight, expert_ids, w_gate, w_up, w_down, delta_in, delta_out
):
    grad_rows, x, g, hid, gpg, gpu, dz, cz = forward(
        rows_in, rows_grad, route_weight, expert_ids, w_gate, w_up, w_down, delta_in, delta_out
    )
    return (grad_rows,) + tuple(weight_grads(x, g, hid, gpg, gpu, dz, cz))


def per_device(
    rows_in, rows_grad, route_weight, expert_ids, w_gate, w_up, w_down, delta_in, delta_out
):
    inputs, cotangent = (
        lax.all_gather(rows_in, "loop", axis=0, tiled=True),
        lax.all_gather(rows_grad, "loop", axis=0, tiled=True),
    )
    gate = jnp.dot(inputs, w_gate, preferred_element_type=jnp.float32)
    up = jnp.dot(inputs, w_up, preferred_element_type=jnp.float32)
    sig = jax.nn.sigmoid(gate)
    hidden = (gate * sig * up).astype(jnp.bfloat16)
    grad_hidden = jnp.dot(cotangent, w_down.T, preferred_element_type=jnp.float32)
    grad_pre_gate = (grad_hidden * up * sig * (1.0 + gate * (1.0 - sig))).astype(jnp.bfloat16)
    grad_pre_up = (grad_hidden * gate * sig).astype(jnp.bfloat16)
    grad_down = jnp.dot(hidden.T, cotangent, preferred_element_type=jnp.float32).astype(
        jnp.bfloat16
    )
    grad_gate = jnp.dot(inputs.T, grad_pre_gate, preferred_element_type=jnp.float32).astype(
        jnp.bfloat16
    )
    grad_up = jnp.dot(inputs.T, grad_pre_up, preferred_element_type=jnp.float32).astype(
        jnp.bfloat16
    )
    owned = delta_in.shape[0]
    expert = lax.axis_index("loop") * owned // RANK
    matched = expert_ids == expert
    coef = jnp.sum(jnp.where(matched, route_weight, jnp.zeros_like(route_weight)), axis=1)
    proj = jnp.dot(inputs, delta_in.T, preferred_element_type=jnp.float32)
    back = jnp.dot(cotangent, delta_out.T, preferred_element_type=jnp.float32)
    grad_z = (coef[:, None] * back).astype(jnp.bfloat16)
    scaled_z = (coef[:, None] * proj).astype(jnp.bfloat16)
    grad_delta_in = jnp.dot(grad_z.T, inputs, preferred_element_type=jnp.float32).astype(
        jnp.bfloat16
    )
    grad_delta_out = jnp.dot(scaled_z.T, cotangent, preferred_element_type=jnp.float32).astype(
        jnp.bfloat16
    )
    delta_rows_term = jnp.dot(grad_z, delta_in, preferred_element_type=jnp.float32)
    partial_value = jnp.dot(grad_pre_gate, w_gate.T, preferred_element_type=jnp.float32)
    partial_value = partial_value + jnp.dot(grad_pre_up, w_up.T, preferred_element_type=jnp.float32)
    partial_value = partial_value + delta_rows_term
    summed = lax.psum_scatter(partial_value, "loop", scatter_dimension=0, tiled=True)
    grad_rows = summed.astype(jnp.bfloat16)
    return (grad_rows, grad_gate, grad_up, grad_down, grad_delta_in, grad_delta_out)


def solution(mesh):
    placed = (
        P(("grp", "loop"), None),
        P(("grp", "loop"), None),
        P("grp", None),
        P("grp", None),
        P(None, "loop"),
        P(None, "loop"),
        P("loop", None),
        P("loop", None),
        P("loop", None),
    )
    device = fused_device if mesh.shape["loop"] == 16 else per_device
    return jax.shard_map(
        device,
        mesh=mesh,
        in_specs=placed,
        out_specs=(
            P(("grp", "loop"), None),
            P("grp", "loop"),
            P("grp", "loop"),
            P(("grp", "loop"), None),
            P(("grp", "loop"), None),
            P(("grp", "loop"), None),
        ),
        check_vma=False,
    )
```
